256 devices in a mesh: ctx: 32 (over x, z), tp: 8 (over y, core).
Axes of the slice: x: 4, y: 4, z: 8, core: 2. Of those that a mesh axis runs over, the one named last changes fastest.
Arguments:
- query_input: bfloat16 [16384, 8192], P('ctx', 'tp'), may hold values from -6 to 6
- key_input: bfloat16 [16384, 8192], P('ctx', 'tp'), may hold values from -6 to 6
- value_input: bfloat16 [16384, 8192], P('ctx', 'tp'), may hold values from -6 to 6
- log_decay: float32 [16384, 64], P('ctx', 'tp'), may hold values from -1 to 0
- norm_gain: float32 [8192], P('tp'), may hold values from 0.1 to 1.9
- cotangent: bfloat16 [16384, 8192], P('ctx', 'tp'), may hold values from -6 to 6
- doc_lengths: int32 [32], replicated, may hold values from 1 to 8192, 16384 in all
Outputs:
- grad_queries: float32 [16384, 8192], P('ctx', 'tp')
- grad_keys: float32 [16384, 8192], P('ctx', 'tp')
- grad_values: float32 [16384, 8192], P('ctx', 'tp')
- grad_gain: float32 [8192], P('tp')
The draws below stay inside these ranges and needn't reach their ends.
Inputs may be any that keep to these rules, and one draw needn't show every extreme that they name: `doc_lengths`: each document has at least one token, the lengths sum to 16384, and the longest has exactly 8192 tokens.
All inputs are finite; a program needn't handle non-finite values.
Results may differ from the reference program's by a relative error of at most 0.0055.
Values sent between devices are 32-bit elements; how exact they have to be, the bound alone decides.
A program may use at most 128 MiB of HBM per device.

```python
import math
import jax
import jax.numpy as jnp
import numpy as np
from jax import lax

HEADS = 64
DH = 128
TOK_DEV = 512
DOCS = 32
SEQUENCE_LENGTH = 16384
DOC_MOST = 8192


def draw_log_decay(key, part):
    key = jax.random.fold_in(key, 7)
    stochastic_seed_pieces = jax.random.split(key, 7)
    fast_share = 0.5
    rough_low = 0.5
    rough_high = 1.5
    fast_heads = jax.random.bernoulli(stochastic_seed_pieces[0], fast_share, (HEADS,))
    fast_rate = jnp.exp(jax.random.uniform(stochastic_seed_pieces[1], (HEADS,), jnp.float32, math.log(1.0 / 50.0), math.log(1.0 / 30.0)))
    slow_rate = jnp.exp(jax.random.uniform(stochastic_seed_pieces[2], (HEADS,), jnp.float32, math.log(0.2), math.log(0.6))) / SEQUENCE_LENGTH
    typical_forget_level = jnp.where(fast_heads, fast_rate, slow_rate)
    accelerator_scaling_factor = jnp.exp(jax.random.uniform(stochastic_seed_pieces[3], (SEQUENCE_LENGTH // TOK_DEV, HEADS), jnp.float32, math.log(0.5), math.log(2.0)))
    accelerator_scaling_factor = jnp.repeat(accelerator_scaling_factor, TOK_DEV, axis=0, total_repeat_length=SEQUENCE_LENGTH)
    forget_noise_spread = jax.random.uniform(stochastic_seed_pieces[4], (SEQUENCE_LENGTH, HEADS), jnp.float32, rough_low, rough_high)
    spike_location = jax.random.bernoulli(stochastic_seed_pieces[5], 2.0 / SEQUENCE_LENGTH, (SEQUENCE_LENGTH, 1))
    forget_strength = jax.random.uniform(stochastic_seed_pieces[6], (SEQUENCE_LENGTH, 1), jnp.float32, 0.22, 0.7)
    return -(typical_forget_level[None, :] * accelerator_scaling_factor * forget_noise_spread) - jnp.where(spike_location, forget_strength, 0.0)


def block_scale(stream_key, extent, cuts, low, largest):
    level, own = 1.0, jax.random.fold_in(stream_key, 6)
    for dim, shards_of in cuts:
        draws = jnp.exp(jax.random.uniform(jax.random.fold_in(own, dim), (shards_of,), jnp.float32, low / len(cuts), largest / len(cuts)))
        level = level * jnp.repeat(draws, extent[dim] // shards_of).reshape([-1 if axis == dim else 1 for axis in range(len(extent))])
    return level


def profile(number_of, total, most, lean):
    portions = [(1 << 20) // math.isqrt(standing ** lean) + 1 for standing in range(2, number_of + 1)]
    surplus, given = total - most - (number_of - 1), [1] * (number_of - 1)
    while surplus > 0:
        free = [i for i in range(number_of - 1) if given[i] < most]
        whole, budget = sum([portions[i] for i in free]), surplus
        for i in free:
            extra = min(most - given[i], max(1, budget * portions[i] // whole), surplus)
            given[i] = given[i] + extra
            surplus = surplus - extra
    return np.array([most] + given)


def ragged(key, count, total, most, lean):
    if count == 2:
        one = jax.random.randint(key, (), max(1, total - most), min(most, total - 1) + 1)
        return jnp.stack([one, total - one])
    lengths = jnp.asarray(profile(count, total, most, lean), jnp.int32)
    couples = (count - 1) // 2
    source_of, taker = lengths[1:1 + 2 * couples:2], lengths[2:2 + 2 * couples:2]
    slack = jnp.minimum(source_of - 1, most - taker)
    moved = jax.random.randint(jax.random.fold_in(key, 1), (couples,), 0, 1 << 20) % (slack + 1)
    lengths = lengths.at[1:1 + 2 * couples:2].set(source_of - moved).at[2:2 + 2 * couples:2].set(taker + moved)
    return lengths[jax.random.permutation(jax.random.fold_in(key, 2), count)]


def bell_draw(own_key, shape, deviation, limit, pieces=(), held_as=jnp.bfloat16):
    entries = deviation * jax.random.normal(own_key, shape, jnp.float32)
    if pieces:
        entries = entries * block_scale(own_key, shape, pieces, -0.22, 0.18)
    return jnp.clip(entries, -limit, limit).astype(held_as)


def setup_inputs(seed: int = 0) -> dict:
    streams_of = jax.random.split(jax.random.key(seed), 8)
    return {
        "query_input": bell_draw(streams_of[0], (SEQUENCE_LENGTH, HEADS * DH), 1.0, 6.0, ((0, 32), (1, 8))),
        "key_input": bell_draw(streams_of[1], (SEQUENCE_LENGTH, HEADS * DH), 1.0, 6.0, ((0, 32), (1, 8))),
        "value_input": bell_draw(streams_of[2], (SEQUENCE_LENGTH, HEADS * DH), 1.0, 6.0, ((0, 32), (1, 8))),
        "log_decay": draw_log_decay(jax.random.fold_in(streams_of[7], 71), 0),
        "norm_gain": jnp.clip(1.0 + 0.18 * jax.random.normal(streams_of[4], (HEADS * DH,), jnp.float32), 0.1, 1.9),
        "cotangent": bell_draw(streams_of[5], (SEQUENCE_LENGTH, HEADS * DH), 1.0, 6.0, ((0, 32), (1, 8))),
        "doc_lengths": ragged(streams_of[6], DOCS, SEQUENCE_LENGTH, DOC_MOST, 2).astype(jnp.int32),
    }


norm_eps = 1e-06

def split_state(state):
    high_part = state.astype(jnp.bfloat16)
    low_part = (state - high_part.astype(jnp.float32)).astype(jnp.bfloat16)
    return (high_part.astype(jnp.float32), low_part.astype(jnp.float32))

def state_product(form, operand, state):
    high_part, low_part = split_state(state)
    return jnp.einsum(form, operand, high_part) + jnp.einsum(form, operand, low_part)

def block_masks(decay_block, seg_block, before):
    length = seg_block.shape[0]
    cumulative = jnp.cumsum(decay_block, axis=0)
    ordinal = jnp.arange(length, dtype=jnp.int32)
    allowed = (seg_block[:, None] == seg_block[None, :]) & (ordinal[:, None] >= ordinal[None, :])
    spread = cumulative.T[:, :, None] - cumulative.T[:, None, :]
    weights = jnp.where(allowed[None], jnp.exp(jnp.where(allowed[None], spread, 0.0)), 0.0)
    linked = seg_block == before
    closing = seg_block == seg_block[-1]
    head_decay = jnp.where(linked[:, None], jnp.exp(cumulative), 0.0)
    tail_decay = jnp.where(closing[:, None], jnp.exp(cumulative[-1][None, :] - cumulative), 0.0)
    through = jnp.where(linked[-1], jnp.exp(cumulative[-1]), 0.0)
    return (weights, head_decay, tail_decay, through)

def forward_block(query_block, key_block, value_block, weights, head_decay, tail_decay, state_in):
    query_wide = query_block.astype(jnp.float32)
    key_wide = key_block.astype(jnp.float32)
    value_wide = value_block.astype(jnp.float32)
    scores = jnp.einsum('thd,shd->hts', query_wide, key_wide)
    probs = (scores * weights).astype(jnp.bfloat16)
    within = jnp.einsum('hts,shd->thd', probs.astype(jnp.float32), value_wide)
    incoming = state_product('thd,hde->the', query_wide, state_in) * head_decay[:, :, None]
    decayed = (value_wide * tail_decay[:, :, None]).astype(jnp.bfloat16)
    local_state = jnp.einsum('shd,she->hde', key_wide, decayed.astype(jnp.float32))
    return (within + incoming, local_state)

def backward_block(query_block, key_block, value_block, grad_block, weights, head_decay, tail_decay, state_in, grad_in):
    query_wide = query_block.astype(jnp.float32)
    key_wide = key_block.astype(jnp.float32)
    value_wide = value_block.astype(jnp.float32)
    grad_wide = grad_block.astype(jnp.float32)
    scores = jnp.einsum('thd,shd->hts', query_wide, key_wide)
    probs = (scores * weights).astype(jnp.bfloat16).astype(jnp.float32)
    grad_scores = jnp.einsum('thd,shd->hts', grad_wide, value_wide)
    grad_probs = (grad_scores * weights).astype(jnp.bfloat16).astype(jnp.float32)
    grad_query = jnp.einsum('hts,shd->thd', grad_probs, key_wide) + state_product('the,hde->thd', grad_wide, state_in) * head_decay[:, :, None]
    grad_key = jnp.einsum('hts,thd->shd', grad_probs, query_wide) + state_product('she,hde->shd', value_wide, grad_in) * tail_decay[:, :, None]
    grad_value = jnp.einsum('hts,thd->shd', probs, grad_wide) + state_product('shd,hde->she', key_wide, grad_in) * tail_decay[:, :, None]
    lifted = (query_wide * head_decay[:, :, None]).astype(jnp.bfloat16)
    emitted = jnp.einsum('thd,the->hde', lifted.astype(jnp.float32), grad_wide)
    return (grad_query, grad_key, grad_value, emitted)

def reference(query_input, key_input, value_input, log_decay, norm_gain, cotangent, doc_lengths):
    blocks = SEQUENCE_LENGTH // TOK_DEV
    shaped = (blocks, TOK_DEV, HEADS, DH)
    query_all = query_input.reshape(shaped)
    key_all = key_input.reshape(shaped)
    value_all = value_input.reshape(shaped)
    decay_all = log_decay.reshape(blocks, TOK_DEV, HEADS)
    starts = (jnp.cumsum(doc_lengths) - doc_lengths).astype(jnp.int32)
    position = jnp.arange(SEQUENCE_LENGTH, dtype=jnp.int32)
    segment = (lax.optimization_barrier(jnp.sum((starts[None, :] <= position[:, None]).astype(jnp.int32), axis=1)) - 1).astype(jnp.int32)
    seg_all = segment.reshape(blocks, TOK_DEV)
    edges = (jnp.arange(blocks, dtype=jnp.int32) * TOK_DEV - 1).astype(jnp.int32)
    before_all = (lax.optimization_barrier(jnp.sum((starts[None, :] <= edges[:, None]).astype(jnp.int32), axis=1)) - 1).astype(jnp.int32)
    zero_state = jnp.zeros((HEADS, DH, DH), jnp.float32)

    def forward_step(state_in, inputs):
        query_block, key_block, value_block, decay_block, seg_block, before = inputs
        weights, head_decay, tail_decay, through = block_masks(decay_block, seg_block, before)
        output, local_state = forward_block(query_block, key_block, value_block, weights, head_decay, tail_decay, state_in)
        return (through[:, None, None] * state_in + local_state, (output, state_in))
    final_state, (outputs, states) = lax.scan(forward_step, zero_state, (query_all, key_all, value_all, decay_all, seg_all, before_all))
    output = outputs.reshape(SEQUENCE_LENGTH, HEADS * DH)
    grad_y = cotangent.astype(jnp.float32)
    total_width = HEADS * DH
    squares = lax.optimization_barrier(jnp.sum(output * output, axis=1))
    crossed = lax.optimization_barrier(jnp.sum(norm_gain[None, :] * grad_y * output, axis=1))
    scaled = 1.0 / jnp.sqrt(squares / total_width + norm_eps)
    cubed = scaled * scaled * scaled
    grad_out = (scaled[:, None] * norm_gain[None, :] * grad_y - output * (cubed * crossed / total_width)[:, None]).astype(jnp.bfloat16)
    grad_gain = lax.optimization_barrier(jnp.sum(grad_y * output * scaled[:, None], axis=0))
    grad_all = grad_out.reshape(shaped)

    def backward_step(grad_in, inputs):
        query_block, key_block, value_block, decay_block, seg_block, before, state_in, grad_block = inputs
        weights, head_decay, tail_decay, through = block_masks(decay_block, seg_block, before)
        grad_query, grad_key, grad_value, emitted = backward_block(query_block, key_block, value_block, grad_block, weights, head_decay, tail_decay, state_in, grad_in)
        return (emitted + through[:, None, None] * grad_in, (grad_query, grad_key, grad_value))
    final_grad, (grad_q_all, grad_k_all, grad_v_all) = lax.scan(backward_step, zero_state, (query_all, key_all, value_all, decay_all, seg_all, before_all, states, grad_all), reverse=True)
    return (grad_q_all.reshape(SEQUENCE_LENGTH, HEADS * DH), grad_k_all.reshape(SEQUENCE_LENGTH, HEADS * DH), grad_v_all.reshape(SEQUENCE_LENGTH, HEADS * DH), grad_gain)
```

```python
import jax
import jax.numpy as jnp
from jax import lax
from jax.sharding import PartitionSpec as P

DH = 128


norm_eps = 1e-06


def spread_slices(state, through, reverse):
    count = lax.axis_size("ctx")
    heads, rows, width = state.shape
    part = rows // count
    pieces = state.reshape(heads, count, part, width).swapaxes(0, 1).reshape(count, heads * part, width)
    extra = jnp.broadcast_to(jnp.pad(through, (0, width - heads))[None, None, :], (count, 1, width))
    got = lax.all_to_all(jnp.concatenate([pieces, extra], axis=1), "ctx", 0, 0, tiled=True)
    blocks = got[:, : heads * part].reshape(count, heads, part, width)
    decay = got[:, heads * part, :heads]
    order = range(count - 1, -1, -1) if reverse else range(count)
    carry = jnp.zeros((heads, part, width), jnp.float32)
    results = [None] * count
    for block in order:
        results[block] = carry
        carry = decay[block][:, None, None] * carry + blocks[block]
    back = jnp.stack(results).reshape(count, heads * part, width)
    back = lax.all_to_all(back, "ctx", 0, 0, tiled=True)
    return back.reshape(count, heads, part, width).swapaxes(0, 1).reshape(heads, rows, width)


def split_state(state):
    high_part = state.astype(jnp.bfloat16)
    low_part = (state - high_part.astype(jnp.float32)).astype(jnp.bfloat16)
    return (high_part, low_part)


def state_product(form, operand, state):
    high_part, low_part = split_state(state)
    first = jnp.einsum(form, operand, high_part, preferred_element_type=jnp.float32)
    return first + jnp.einsum(form, operand, low_part, preferred_element_type=jnp.float32)


def block_masks(decay_block, seg_block, before):
    length = seg_block.shape[0]
    cumulative = jnp.cumsum(decay_block, axis=0)
    ordinal = jnp.arange(length, dtype=jnp.int32)
    allowed = (seg_block[:, None] == seg_block[None, :]) & (ordinal[:, None] >= ordinal[None, :])
    spread = cumulative.T[:, :, None] - cumulative.T[:, None, :]
    weights = jnp.where(allowed[None], jnp.exp(jnp.where(allowed[None], spread, 0.0)), 0.0)
    linked = seg_block == before
    closing = seg_block == seg_block[-1]
    head_decay = jnp.where(linked[:, None], jnp.exp(cumulative), 0.0)
    tail_decay = jnp.where(closing[:, None], jnp.exp(cumulative[-1][None, :] - cumulative), 0.0)
    through = jnp.where(linked[-1], jnp.exp(cumulative[-1]), 0.0)
    return (weights, head_decay, tail_decay, through)


def local(query_input, key_input, value_input, log_decay, norm_gain, cotangent, doc_lengths):
    row_count = query_input.shape[0]
    head_count = query_input.shape[1] // DH
    query_block = query_input.reshape(row_count, head_count, DH)
    key_block = key_input.reshape(row_count, head_count, DH)
    value_block = value_input.reshape(row_count, head_count, DH)
    offset = lax.axis_index("ctx") * row_count
    starts = jnp.cumsum(doc_lengths) - doc_lengths
    position = offset + jnp.arange(row_count, dtype=jnp.int32)
    segment = jnp.sum((starts[None, :] <= position[:, None]).astype(jnp.int32), axis=1) - 1
    before = jnp.sum((starts <= offset - 1).astype(jnp.int32)) - 1
    weights, head_decay, tail_decay, through = block_masks(log_decay, segment, before)
    scores = jnp.einsum("thd,shd->hts", query_block, key_block, preferred_element_type=jnp.float32)
    probs = (scores * weights).astype(jnp.bfloat16)
    within = jnp.einsum("hts,shd->thd", probs, value_block, preferred_element_type=jnp.float32)
    decayed = (value_block.astype(jnp.float32) * tail_decay[:, :, None]).astype(jnp.bfloat16)
    local_state = jnp.einsum("shd,she->hde", key_block, decayed, preferred_element_type=jnp.float32)
    state_in = spread_slices(local_state, through, False)
    incoming = state_product("thd,hde->the", query_block, state_in) * head_decay[:, :, None]
    output = (within + incoming).reshape(row_count, head_count * DH)
    grad_y = cotangent.astype(jnp.float32)
    squares = jnp.sum(output * output, axis=1)
    crossed = jnp.sum(norm_gain[None, :] * grad_y * output, axis=1)
    squares, crossed = lax.psum(jnp.stack([squares, crossed]), "tp")
    total_width = head_count * DH * lax.axis_size("tp")
    scaled = 1.0 / jnp.sqrt(squares / total_width + norm_eps)
    cubed = scaled * scaled * scaled
    grad_out = (
        scaled[:, None] * norm_gain[None, :] * grad_y
        - output * (cubed * crossed / total_width)[:, None]
    ).astype(jnp.bfloat16)
    grad_gain = lax.psum(jnp.sum(grad_y * output * scaled[:, None], axis=0), "ctx")
    grad_block = grad_out.reshape(row_count, head_count, DH)
    lifted = (query_block.astype(jnp.float32) * head_decay[:, :, None]).astype(jnp.bfloat16)
    emitted = jnp.einsum("thd,the->hde", lifted, grad_block, preferred_element_type=jnp.float32)
    grad_in = spread_slices(emitted, through, True)
    grad_scores = jnp.einsum(
        "thd,shd->hts", grad_block, value_block, preferred_element_type=jnp.float32
    )
    grad_probs = (grad_scores * weights).astype(jnp.bfloat16)
    grad_query = jnp.einsum(
        "hts,shd->thd", grad_probs, key_block, preferred_element_type=jnp.float32
    )
    grad_query = (
        grad_query + state_product("the,hde->thd", grad_block, state_in) * head_decay[:, :, None]
    )
    grad_key = jnp.einsum(
        "hts,thd->shd", grad_probs, query_block, preferred_element_type=jnp.float32
    )
    grad_key = (
        grad_key + state_product("she,hde->shd", value_block, grad_in) * tail_decay[:, :, None]
    )
    grad_value = jnp.einsum("hts,thd->shd", probs, grad_block, preferred_element_type=jnp.float32)
    grad_value = (
        grad_value + state_product("shd,hde->she", key_block, grad_in) * tail_decay[:, :, None]
    )
    flat = (row_count, head_count * DH)
    return (grad_query.reshape(flat), grad_key.reshape(flat), grad_value.reshape(flat), grad_gain)


def solution(mesh):
    placed = (
        P("ctx", "tp"),
        P("ctx", "tp"),
        P("ctx", "tp"),
        P("ctx", "tp"),
        P("tp"),
        P("ctx", "tp"),
        P(),
    )
    return jax.shard_map(
        local,
        mesh=mesh,
        in_specs=placed,
        out_specs=(P("ctx", "tp"), P("ctx", "tp"), P("ctx", "tp"), P("tp")),
        check_vma=False,
    )
```

```python
import jax
import jax.numpy as jnp
from jax import lax
from jax.experimental import pallas as pl
from jax.experimental.pallas import tpu as pltpu
from jax.sharding import PartitionSpec as P

DH = 128
HEADS = 8
TOK = 512
ROWS = 4
COLS = 8
PEERS = 8
PART = DH // COLS
CHUNKS = 2
GROUP = HEADS // CHUNKS
HALF = TOK // 2
WIDTH = HEADS * DH * PEERS
norm_eps = 1e-06
MESH = pl.DeviceIdType.MESH
F32 = jnp.float32
BF16 = jnp.bfloat16

NN = (((1,), (0,)), ((), ()))
NT = (((1,), (1,)), ((), ()))
TN = (((0,), (0,)), ((), ()))


def mm(a, b, form):
    return lax.dot_general(a, b, form, preferred_element_type=F32)


def cols_of(h):
    return pl.ds(pl.multiple_of(h * DH, DH), DH)


def split_state(state):
    high = state.astype(BF16)
    return high, (state - high.astype(F32)).astype(BF16)


def twice(a):
    return jnp.concatenate([a, a], axis=1)


def kernel(
    docs, q_hbm, k_hbm, v_hbm, dec_ref, gain_ref, dy_hbm,
    gq_hbm, gk_hbm, gv_hbm, gg_ref,
    q, k, v, dy, go, outw, gqs, gks, gvs, weights, probs, gps, bias,
    cum_rows, cum_b, head_b, tail_b, acc_sq, acc_cr, scale_b, coef_b,
    thr_own, thr, row_own, row_got,
    f_loc, f_got, f_tot, f_tgot, f_ret, f_state,
    b_loc, b_got, b_tot, b_tgot, b_ret, b_state,
    tp_own, tp_got, gz_own, gz_got, gx_own, gx_got,
    in_sem, out_sem, thr_s, thr_r, row_s, row_r,
    fa_s, fa_r, fx_s, fx_r, fb_s, fb_r,
    ba_s, ba_r, bx_s, bx_r, bb_s, bb_r,
    tp_s, tp_r, gz_s, gz_r, gx_s, gx_r,
):
    c = lax.axis_index("ctx")
    t = lax.axis_index("tp")
    x = c // COLS
    z = lax.rem(c, COLS)

    def z_dev(i):
        return (x * COLS + lax.rem(z + i, COLS), t)

    def x_dev(i):
        return (lax.rem(x + i, ROWS) * COLS + z, t)

    def t_dev(i):
        return (c, lax.rem(t + i, PEERS))

    def load(i, src, dst):
        return pltpu.make_async_copy(src, dst, in_sem.at[i])

    loads = [load(0, k_hbm, k), load(1, v_hbm, v), load(2, q_hbm, q), load(3, dy_hbm, dy)]
    for cp in loads:
        cp.start()

    barrier = pltpu.get_barrier_semaphore()
    others = [z_dev(i) for i in range(1, COLS)]
    others += [x_dev(i) for i in range(1, ROWS)]
    others += [t_dev(i) for i in range(1, PEERS)]
    for other in others:
        pl.semaphore_signal(barrier, inc=1, device_id=other, device_id_type=MESH)

    pending = []

    def remote(src, dst, ss, rs, dev):
        cp = pltpu.make_async_remote_copy(
            src_ref=src, dst_ref=dst, send_sem=ss, recv_sem=rs, device_id=dev, device_id_type=MESH
        )
        cp.start()
        pending.append(cp)
        return cp

    offset = c * TOK
    pos = offset + lax.broadcasted_iota(jnp.int32, (HEADS, TOK), 1)

    def doc_step(d, carry):
        start, low, low_last = carry
        low = jnp.where(pos >= start, start, low)
        low_last = jnp.where(offset + TOK - 1 >= start, start, low_last)
        return start + docs[d], low, low_last

    zero = jnp.int32(0)
    _, low, low_last = lax.fori_loop(
        0, docs.shape[0], doc_step, (zero, jnp.zeros((HEADS, TOK), jnp.int32), zero)
    )
    lane = lax.broadcasted_iota(jnp.int32, (HEADS, TOK), 1)
    cum = dec_ref[...]
    step = 1
    while step < TOK:
        cum = cum + jnp.where(lane >= step, pltpu.roll(cum, step, 1), 0.0)
        step *= 2
    cum_rows[...] = cum
    head = jnp.where(low < offset, jnp.exp(cum), 0.0)
    tail = jnp.where(pos >= low_last, jnp.exp(cum[:, TOK - 1:] - cum), 0.0)
    through = jnp.broadcast_to(head[:, TOK - 1:], (HEADS, DH))
    thr_own[...] = through
    thr[z] = through
    first = (low - offset).astype(F32)
    stacked = jnp.concatenate(
        [cum, head, tail, first, jnp.zeros((DH - 4 * HEADS, TOK), F32)], axis=0
    )
    columns = stacked.T
    for h in range(HEADS):
        at = 2 * HEADS + h
        tail_b[h] = jnp.broadcast_to(columns[:, at:at + 1], (TOK, DH))

    def scatter(loc, got, ss, rs, ch):
        hs = pl.ds(ch * GROUP, GROUP)
        sent = []
        for i in range(1, COLS):
            p = lax.rem(z + i, COLS)
            sent.append(remote(loc.at[p, hs], got.at[z, hs], ss.at[ch, i], rs.at[ch, i], z_dev(i)))
        got[z, hs] = loc[z, hs]
        return sent

    def arrive(copies):
        for cp in copies:
            cp.wait_recv()

    def local_state(h, _):
        hc = cols_of(h)
        decayed = (v[:, hc].astype(F32) * tail_b[h]).astype(BF16)
        f_loc[:, h] = mm(k[:, hc], decayed, TN).reshape(COLS, PART, DH)
        return 0

    loads[0].wait()
    loads[1].wait()
    f_a = [None] * CHUNKS
    f_t = [None] * CHUNKS
    f_b = [None] * CHUNKS
    for ch in range(CHUNKS):
        lax.fori_loop(ch * GROUP, (ch + 1) * GROUP, local_state, 0)
        if ch == 0:
            pl.semaphore_wait(barrier, len(others))
            thr_cp = [
                remote(thr_own, thr.at[z], thr_s.at[i], thr_r.at[i], z_dev(i)) for i in range(1, COLS)
            ]
        f_a[ch] = scatter(f_loc, f_got, fa_s, fa_r, ch)

    for h in range(HEADS):
        cum_b[h] = jnp.broadcast_to(columns[:, h:h + 1], (TOK, DH))
        at = HEADS + h
        head_b[h] = jnp.broadcast_to(columns[:, at:at + 1], (TOK, DH))
    at = 3 * HEADS
    row = lax.broadcasted_iota(jnp.int32, (TOK, TOK), 0)
    col = lax.broadcasted_iota(jnp.int32, (TOK, TOK), 1)
    begin = columns[:, at:at + 1].astype(jnp.int32)
    bias[...] = jnp.where((col >= begin) & (col <= row), 0.0, -1e30)
    loads[2].wait()
    loads[3].wait()

    def within(h, _):
        hc = cols_of(h)
        for i in range(2):
            n = HALF * (i + 1)
            ts = slice(HALF * i, n)
            scores = mm(q[ts, hc], k[:n, hc], NT)
            decay = jnp.concatenate([cum_b[h, ts]] * (n // DH), axis=1)
            spread = decay - cum_rows[pl.ds(h, 1), :n]
            w = jnp.exp(spread + bias[ts, :n])
            p = (scores * w).astype(BF16)
            weights[h, ts, :n] = w
            probs[h, ts, :n] = p
            outw[ts, hc] = mm(p, v[:n, hc], NN)
        return 0

    def scan_local(got, ret, tot, ch, order):
        def body(h, _):
            carry = jnp.zeros((PART, DH), F32)
            for b in order:
                ret[b, h] = carry
                carry = thr[b, pl.ds(h, 1), :] * carry + got[b, h]
            tot[h] = carry
            return 0

        lax.fori_loop(ch * GROUP, (ch + 1) * GROUP, body, 0)

    def scan_rows(ret, tgot, ch, order, near, far, at):
        def body(h, _):
            enter = tgot[0, h] * near + (row_got[at, pl.ds(h, 1), :] * far) * tgot[1, h]
            for b in order:
                ret[b, h] = ret[b, h] + enter
                enter = thr[b, pl.ds(h, 1), :] * enter
            return 0

        lax.fori_loop(ch * GROUP, (ch + 1) * GROUP, body, 0)

    def send_totals(tot, tgot, ss, rs, ch, steps):
        hs = pl.ds(ch * GROUP, GROUP)
        return [
            remote(tot.at[hs], tgot.at[j, hs], ss.at[ch, j], rs.at[ch, j], x_dev(i))
            for j, i in enumerate(steps)
        ]

    forth = range(COLS)
    back = range(COLS - 1, -1, -1)

    lax.fori_loop(0, 2, within, 0)
    arrive(thr_cp)
    total = thr[0]
    for b in range(1, COLS):
        total = total * thr[b]
    row_own[...] = total
    row_cp = [
        remote(row_own, row_got.at[j], row_s.at[j], row_r.at[j], x_dev(i)) for j, i in enumerate((1, 3))
    ]
    for ch in range(CHUNKS):
        arrive(f_a[ch])
        scan_local(f_got, f_ret, f_tot, ch, forth)
        f_t[ch] = send_totals(f_tot, f_tgot, fx_s, fx_r, ch, (1, 2))
        lax.fori_loop(2 + 2 * ch, 4 + 2 * ch, within, 0)
    near = jnp.where(x >= 1, 1.0, 0.0)
    far = jnp.where(x >= 2, 1.0, 0.0)
    arrive(row_cp)
    for ch in range(CHUNKS):
        arrive(f_t[ch])
        scan_rows(f_ret, f_tgot, ch, forth, near, far, 0)
        f_b[ch] = scatter(f_ret, f_state, fb_s, fb_r, ch)
    lax.fori_loop(2 + 2 * CHUNKS, HEADS, within, 0)

    acc_sq[...] = jnp.zeros_like(acc_sq)
    acc_cr[...] = jnp.zeros_like(acc_cr)

    def incoming(h, _):
        hc = cols_of(h)
        high, low_part = split_state(f_state[:, h].reshape(DH, DH))
        got = mm(twice(q[:, hc]), jnp.concatenate([high, low_part], axis=0), NN)
        o = outw[:, hc] + got * head_b[h]
        outw[:, hc] = o
        acc_sq[...] += o * o
        acc_cr[...] += gain_ref[pl.ds(h, 1), :] * dy[:, hc].astype(F32) * o
        return 0

    for ch in range(CHUNKS):
        arrive(f_b[ch])
        lax.fori_loop(ch * GROUP, (ch + 1) * GROUP, incoming, 0)

    ones = jnp.ones((HEADS, DH), F32)

    def row_sums(acc):
        return lax.dot_general(
            ones, acc[...], NT, precision=lax.Precision.HIGHEST, preferred_element_type=F32
        )

    sub = lax.broadcasted_iota(jnp.int32, (HEADS, TOK), 0)
    sums = jnp.where(sub == 0, row_sums(acc_sq), row_sums(acc_cr))
    tp_own[...] = sums
    tp_got[t] = sums
    tp_cp = [
        remote(tp_own, tp_got.at[t], tp_s.at[i], tp_r.at[i], t_dev(i)) for i in range(1, PEERS)
    ]
    arrive(tp_cp)
    sums = tp_got[0]
    for i in range(1, PEERS):
        sums = sums + tp_got[i]
    scaled = 1.0 / jnp.sqrt(sums[0:1] / WIDTH + norm_eps)
    coef = scaled * scaled * scaled * sums[1:2] / WIDTH
    stacked = jnp.concatenate(
        [jnp.broadcast_to(scaled, (HEADS, TOK)), jnp.broadcast_to(coef, (HEADS, TOK)),
         jnp.zeros((DH - 2 * HEADS, TOK), F32)], axis=0
    )
    norm_columns = stacked.T
    scale_b[...] = jnp.broadcast_to(norm_columns[:, 0:1], (TOK, DH))
    coef_b[...] = jnp.broadcast_to(norm_columns[:, HEADS:HEADS + 1], (TOK, DH))

    def emit(h, _):
        hc = cols_of(h)
        o = outw[:, hc]
        dyh = dy[:, hc].astype(F32)
        sc = scale_b[...]
        g = (sc * gain_ref[pl.ds(h, 1), :] * dyh - o * coef_b[...]).astype(BF16)
        go[:, hc] = g
        gz_own[pl.ds(h, 1), :] = jnp.sum(dyh * o * sc, axis=0, keepdims=True)
        lifted = (q[:, hc].astype(F32) * head_b[h]).astype(BF16)
        b_loc[:, h] = mm(lifted, g, TN).reshape(COLS, PART, DH)
        return 0

    b_a = [None] * CHUNKS
    b_t = [None] * CHUNKS
    b_b = [None] * CHUNKS
    for ch in range(CHUNKS):
        lax.fori_loop(ch * GROUP, (ch + 1) * GROUP, emit, 0)
        b_a[ch] = scatter(b_loc, b_got, ba_s, ba_r, ch)
    gz_got[z] = gz_own[...]
    gz_cp = [
        remote(gz_own, gz_got.at[z], gz_s.at[i], gz_r.at[i], z_dev(i)) for i in range(1, COLS)
    ]

    def grads(h, _):
        hc = cols_of(h)
        high, low_part = split_state(f_state[:, h].reshape(DH, DH))
        state = jnp.concatenate([high, low_part], axis=1)
        for i in range(2):
            n = HALF * (i + 1)
            ts = slice(HALF * i, n)
            g = go[ts, hc]
            gp = (mm(g, v[:n, hc], NT) * weights[h, ts, :n]).astype(BF16)
            gps[ts, :n] = gp
            across = mm(twice(g), state, NT) * head_b[h, ts]
            gqs[ts, hc] = mm(gp, k[:n, hc], NN) + across
        for j in range(2):
            rs = slice(HALF * j, TOK)
            ss = slice(HALF * j, HALF * (j + 1))
            gks[ss, hc] = mm(gps[rs, ss], q[rs, hc], TN)
            gvs[ss, hc] = mm(probs[h, rs, ss], go[rs, hc], TN)
        return 0

    def store(i, src, dst, hs):
        cp = pltpu.make_async_copy(src.at[:, hs], dst.at[:, hs], out_sem.at[i])
        cp.start()
        return cp

    lax.fori_loop(0, 2, grads, 0)
    for ch in range(CHUNKS):
        arrive(b_a[ch])
        scan_local(b_got, b_ret, b_tot, ch, back)
        b_t[ch] = send_totals(b_tot, b_tgot, bx_s, bx_r, ch, (3, 2))
        lax.fori_loop(2 + 2 * ch, 4 + 2 * ch, grads, 0)
    arrive(gz_cp)
    part = gz_got[0]
    for b in range(1, COLS):
        part = part + gz_got[b]
    gx_own[...] = part
    gx_got[x] = part
    gx_cp = [
        remote(gx_own, gx_got.at[x], gx_s.at[i], gx_r.at[i], x_dev(i)) for i in range(1, ROWS)
    ]
    near = jnp.where(x <= ROWS - 2, 1.0, 0.0)
    far = jnp.where(x <= ROWS - 3, 1.0, 0.0)
    for ch in range(CHUNKS):
        arrive(b_t[ch])
        scan_rows(b_ret, b_tgot, ch, back, near, far, 1)
        b_b[ch] = scatter(b_ret, b_state, bb_s, bb_r, ch)
    lax.fori_loop(2 + 2 * CHUNKS, HEADS, grads, 0)
    stores = [store(0, gqs, gq_hbm, pl.ds(0, HEADS * DH))]
    arrive(gx_cp)
    part = gx_got[0]
    for b in range(1, ROWS):
        part = part + gx_got[b]
    gg_ref[...] = part

    def finish(h, _):
        hc = cols_of(h)
        high, low_part = split_state(b_state[:, h].reshape(DH, DH))
        decay = tail_b[h]
        gks[:, hc] += mm(twice(v[:, hc]), jnp.concatenate([high, low_part], axis=1), NT) * decay
        gvs[:, hc] += mm(twice(k[:, hc]), jnp.concatenate([high, low_part], axis=0), NN) * decay
        return 0

    for ch in range(CHUNKS):
        arrive(b_b[ch])
        lax.fori_loop(ch * GROUP, (ch + 1) * GROUP, finish, 0)
        hs = pl.ds(ch * GROUP * DH, GROUP * DH)
        stores.append(store(1 + 2 * ch, gks, gk_hbm, hs))
        stores.append(store(2 + 2 * ch, gvs, gv_hbm, hs))
    for cp in pending:
        cp.wait_send()
    for cp in stores:
        cp.wait()


def local(query_input, key_input, value_input, log_decay, norm_gain, cotangent, doc_lengths):
    flat = (TOK, HEADS * DH)
    vmem = pltpu.VMEM
    dma = pltpu.SemaphoreType.DMA
    states = [
        vmem((COLS, HEADS, PART, DH), F32),
        vmem((COLS, HEADS, PART, DH), F32),
        vmem((HEADS, PART, DH), F32),
        vmem((2, HEADS, PART, DH), F32),
        vmem((COLS, HEADS, PART, DH), F32),
        vmem((COLS, HEADS, PART, DH), F32),
    ]
    tile = vmem((HEADS, DH), F32)
    per_head = vmem((HEADS, TOK, DH), F32)
    column = vmem((TOK, DH), F32)
    out = jax.ShapeDtypeStruct(flat, F32)
    anywhere = pl.BlockSpec(memory_space=pl.ANY)
    in_vmem = pl.BlockSpec(memory_space=pltpu.VMEM)
    chunk_sems = [
        dma((CHUNKS, COLS)), dma((CHUNKS, COLS)),
        dma((CHUNKS, 2)), dma((CHUNKS, 2)),
        dma((CHUNKS, COLS)), dma((CHUNKS, COLS)),
    ]
    gq, gk, gv, gg = pl.pallas_call(
        kernel,
        out_shape=(out, out, out, jax.ShapeDtypeStruct((HEADS, DH), F32)),
        in_specs=[
            pl.BlockSpec(memory_space=pltpu.SMEM), anywhere, anywhere, anywhere, in_vmem, in_vmem, anywhere,
        ],
        out_specs=(anywhere, anywhere, anywhere, in_vmem),
        scratch_shapes=[
            vmem(flat, BF16), vmem(flat, BF16), vmem(flat, BF16), vmem(flat, BF16), vmem(flat, BF16),
            vmem(flat, F32), vmem(flat, F32), vmem(flat, F32), vmem(flat, F32),
            vmem((HEADS, TOK, TOK), F32), vmem((HEADS, TOK, TOK), BF16), vmem((TOK, TOK), BF16),
            vmem((TOK, TOK), F32),
            vmem((HEADS, TOK), F32), per_head, per_head, per_head, column, column, column, column,
            tile, vmem((COLS, HEADS, DH), F32), tile, vmem((2, HEADS, DH), F32),
            *states, *states,
            vmem((HEADS, TOK), F32), vmem((PEERS, HEADS, TOK), F32),
            tile, vmem((COLS, HEADS, DH), F32), tile, vmem((ROWS, HEADS, DH), F32),
            dma((4,)), dma((1 + 2 * CHUNKS,)), dma((COLS,)), dma((COLS,)), dma((2,)), dma((2,)),
            *chunk_sems, *chunk_sems,
            dma((PEERS,)), dma((PEERS,)), dma((COLS,)), dma((COLS,)), dma((ROWS,)), dma((ROWS,)),
        ],
        compiler_params=pltpu.CompilerParams(
            collective_id=0, has_side_effects=True, vmem_limit_bytes=60 << 20
        ),
        cost_estimate=pl.CostEstimate(flops=5 << 30, bytes_accessed=10 << 20, transcendentals=2 << 20),
        name="attention_backward",
    )(
        doc_lengths, query_input, key_input, value_input, log_decay.T,
        norm_gain.reshape(HEADS, DH), cotangent,
    )
    return (gq, gk, gv, gg.reshape(HEADS * DH))


def solution(mesh):
    placed = (
        P("ctx", "tp"),
        P("ctx", "tp"),
        P("ctx", "tp"),
        P("ctx", "tp"),
        P("tp"),
        P("ctx", "tp"),
        P(),
    )
    return jax.shard_map(
        local,
        mesh=mesh,
        in_specs=placed,
        out_specs=(P("ctx", "tp"), P("ctx", "tp"), P("ctx", "tp"), P("tp")),
        check_vma=False,
    )
```

```python
import jax
import jax.numpy as jnp
from jax import lax
from jax.experimental import pallas as pl
from jax.experimental.pallas import tpu as pltpu
from jax.sharding import PartitionSpec as P

DH = 128
HEADS = 8
TOK = 512
ROWS = 4
COLS = 8
PEERS = 8
PART = DH // COLS
CHUNKS = 4
GROUP = HEADS // CHUNKS
HALF = TOK // 2
WIDTH = HEADS * DH * PEERS
norm_eps = 1e-06
MESH = pl.DeviceIdType.MESH
RING = (4, 3, 5, 2, 6, 1, 7)
LINE = (2, 1, 3)
TEAM = (4, 5, 3, 2, 6, 7, 1)
F32 = jnp.float32
BF16 = jnp.bfloat16

NN = (((1,), (0,)), ((), ()))
NT = (((1,), (1,)), ((), ()))
TN = (((0,), (0,)), ((), ()))


def mm(a, b, form):
    return lax.dot_general(a, b, form, preferred_element_type=F32)


def cols_of(h):
    return pl.ds(pl.multiple_of(h * DH, DH), DH)


def split_state(state):
    high = state.astype(BF16)
    return high, (state - high.astype(F32)).astype(BF16)


def twice(a):
    return jnp.concatenate([a, a], axis=1)


def kernel(
    docs, q_hbm, k_hbm, v_hbm, dec_hbm, gain_hbm, dy_hbm,
    gqs, gks, gvs, gg_ref, b_state, columns, k, v,
    q, dy, go, outw, weights, probs, gps, bias, dec, gain,
    cum_rows, cum_b, head_b, tail_b, acc_sq, acc_cr, scale_b, coef_b,
    thr_own, thr, row_own, row_got,
    f_loc, f_got, f_tot, f_tgot, f_ret, f_state,
    b_loc, b_got, b_tot, b_tgot, b_ret,
    tp_own, tp_got, gz_own, gz_got, gx_own, gx_got,
    in_sem, send_sem, recv_sem, fa_r, fx_r, fb_r, ba_r, bx_r, bb_r,
):
    c = lax.axis_index("ctx")
    t = lax.axis_index("tp")
    x = c // COLS
    z = lax.rem(c, COLS)

    def z_dev(i):
        return (x * COLS + lax.rem(z + i, COLS), t)

    def x_dev(i):
        return (lax.rem(x + i, ROWS) * COLS + z, t)

    def t_dev(i):
        return (c, lax.rem(t + i, PEERS))

    def load(i, src, dst):
        cp = pltpu.make_async_copy(src, dst, in_sem.at[i])
        cp.start()
        return cp

    small = [load(0, dec_hbm, dec), load(1, gain_hbm, gain)]
    pair = []
    for ch in range(CHUNKS):
        hs = pl.ds(ch * GROUP * DH, GROUP * DH)
        pair.append(
            [load(2 + 2 * ch, k_hbm.at[:, hs], k.at[:, hs]), load(3 + 2 * ch, v_hbm.at[:, hs], v.at[:, hs])]
        )

    barrier = pltpu.get_barrier_semaphore()
    others = [z_dev(i) for i in RING] + [x_dev(i) for i in LINE] + [t_dev(i) for i in TEAM]
    for other in others:
        pl.semaphore_signal(barrier, inc=1, device_id=other, device_id_type=MESH)

    def remote(src, dst, phase, rs, dev):
        return pltpu.make_async_remote_copy(
            src_ref=src, dst_ref=dst, send_sem=send_sem.at[phase], recv_sem=rs, device_id=dev, device_id_type=MESH
        )

    def arrive(view, rs):
        remote(view, view, 0, rs, others[0]).wait_recv()

    def sent(view, phase):
        remote(view, view, phase, recv_sem.at[0], others[0]).wait_send()

    offset = c * TOK
    pos = offset + lax.broadcasted_iota(jnp.int32, (HEADS, TOK), 1)

    def doc_step(d, carry):
        start, low, low_last = carry
        low = jnp.where(pos >= start, start, low)
        low_last = jnp.where(offset + TOK - 1 >= start, start, low_last)
        return start + docs[d], low, low_last

    zero = jnp.int32(0)
    _, low, low_last = lax.fori_loop(
        0, docs.shape[0], doc_step, (zero, jnp.zeros((HEADS, TOK), jnp.int32), zero)
    )
    lane = lax.broadcasted_iota(jnp.int32, (HEADS, TOK), 1)
    small[0].wait()
    cum = dec[...]
    step = 1
    while step < TOK:
        cum = cum + jnp.where(lane >= step, pltpu.roll(cum, step, 1), 0.0)
        step *= 2
    cum_rows[...] = cum
    head = jnp.where(low < offset, jnp.exp(cum), 0.0)
    tail = jnp.where(pos >= low_last, jnp.exp(cum[:, TOK - 1:] - cum), 0.0)
    through = jnp.broadcast_to(head[:, TOK - 1:], (HEADS, DH))
    thr_own[...] = through
    thr[z] = through
    first = (low - offset).astype(F32)
    stacked = jnp.concatenate(
        [cum, head, tail, first, jnp.zeros((DH - 4 * HEADS, TOK), F32)], axis=0
    )
    columns[...] = stacked.T
    for h in range(HEADS):
        at = 2 * HEADS + h
        tail_b[h] = jnp.broadcast_to(columns[:, at:at + 1], (TOK, DH))

    def scatter(loc, got, phase, rs, ch):
        hs = pl.ds(ch * GROUP, GROUP)
        for i in RING:
            p = lax.rem(z + i, COLS)
            remote(loc.at[p, hs], got.at[z, hs], phase, rs.at[ch], z_dev(i)).start()
        got[z, hs] = loc[z, hs]

    def gather(got, rs, ch):
        arrive(got.at[pl.ds(0, COLS - 1), pl.ds(ch * GROUP, GROUP)], rs.at[ch])

    def local_state(h, _):
        hc = cols_of(h)
        decayed = (v[:, hc].astype(F32) * tail_b[h]).astype(BF16)
        f_loc[:, h] = mm(k[:, hc], decayed, TN).reshape(COLS, PART, DH)
        return 0

    for ch in range(CHUNKS):
        for cp in pair[ch]:
            cp.wait()
        lax.fori_loop(ch * GROUP, (ch + 1) * GROUP, local_state, 0)
        if ch == 0:
            pl.semaphore_wait(barrier, len(others))
            for i in RING:
                remote(thr_own, thr.at[z], 0, recv_sem.at[0], z_dev(i)).start()
        scatter(f_loc, f_got, 1, fa_r, ch)
    late = [load(2 + 2 * CHUNKS, q_hbm, q), load(3 + 2 * CHUNKS, dy_hbm, dy)]

    for h in range(HEADS):
        cum_b[h] = jnp.broadcast_to(columns[:, h:h + 1], (TOK, DH))
        at = HEADS + h
        head_b[h] = jnp.broadcast_to(columns[:, at:at + 1], (TOK, DH))
    at = 3 * HEADS
    row = lax.broadcasted_iota(jnp.int32, (TOK, TOK), 0)
    col = lax.broadcasted_iota(jnp.int32, (TOK, TOK), 1)
    begin = columns[:, at:at + 1].astype(jnp.int32)
    bias[...] = jnp.where((col >= begin) & (col <= row), 0.0, -1e30)
    late[0].wait()

    def within(h, _):
        hc = cols_of(h)
        for i in range(2):
            n = HALF * (i + 1)
            ts = slice(HALF * i, n)
            scores = mm(q[ts, hc], k[:n, hc], NT)
            decay = jnp.concatenate([cum_b[h, ts]] * (n // DH), axis=1)
            spread = decay - cum_rows[pl.ds(h, 1), :n]
            w = jnp.exp(spread + bias[ts, :n])
            p = (scores * w).astype(BF16)
            weights[h, ts, :n] = w
            probs[h, ts, :n] = p
            outw[ts, hc] = mm(p, v[:n, hc], NN)
        return 0

    def scan_local(got, ret, tot, ch, order):
        def body(h, _):
            carry = jnp.zeros((PART, DH), F32)
            for b in order:
                ret[b, h] = carry
                carry = thr[b, pl.ds(h, 1), :] * carry + got[b, h]
            tot[h] = carry
            return 0

        lax.fori_loop(ch * GROUP, (ch + 1) * GROUP, body, 0)

    def scan_rows(ret, tgot, ch, order, near, far, at):
        def body(h, _):
            enter = tgot[0, h] * near + (row_got[at, pl.ds(h, 1), :] * far) * tgot[1, h]
            for b in order:
                ret[b, h] = ret[b, h] + enter
                enter = thr[b, pl.ds(h, 1), :] * enter
            return 0

        lax.fori_loop(ch * GROUP, (ch + 1) * GROUP, body, 0)

    def send_totals(tot, tgot, phase, rs, ch, steps):
        hs = pl.ds(ch * GROUP, GROUP)
        for j, i in reversed(list(enumerate(steps))):
            remote(tot.at[hs], tgot.at[j, hs], phase, rs.at[ch], x_dev(i)).start()

    forth = range(COLS)
    back = range(COLS - 1, -1, -1)

    lax.fori_loop(0, 3, within, 0)
    arrive(thr.at[pl.ds(0, COLS - 1)], recv_sem.at[0])
    total = thr[0]
    for b in range(1, COLS):
        total = total * thr[b]
    row_own[...] = total
    for j, i in enumerate((1, 3)):
        remote(row_own, row_got.at[j], 2, recv_sem.at[1], x_dev(i)).start()

    def scan(state, phase, sems, order, steps, near, far, at, fill, first_fill):
        got, ret, tot, tgot, back_to = state
        a_r, x_r, b_r = sems

        def give(ch):
            arrive(tgot.at[:, pl.ds(ch * GROUP, GROUP)], x_r.at[ch])
            scan_rows(ret, tgot, ch, order, near, far, at)
            scatter(ret, back_to, phase + 1, b_r, ch)

        for ch in range(CHUNKS):
            gather(got, a_r, ch)
            scan_local(got, ret, tot, ch, order)
            send_totals(tot, tgot, phase, x_r, ch, steps)
            lax.fori_loop(first_fill + ch, first_fill + ch + 1, fill, 0)
            if ch == 0:
                arrive(row_got, recv_sem.at[1]) if at == 0 else None
            if ch >= 1:
                give(ch - 1)
        give(CHUNKS - 1)
        lax.fori_loop(first_fill + CHUNKS, HEADS, fill, 0)

    scan(
        (f_got, f_ret, f_tot, f_tgot, f_state), 3, (fa_r, fx_r, fb_r), forth, (1, 2),
        jnp.where(x >= 1, 1.0, 0.0), jnp.where(x >= 2, 1.0, 0.0), 0, within, 3,
    )

    acc_sq[...] = jnp.zeros_like(acc_sq)
    acc_cr[...] = jnp.zeros_like(acc_cr)

    def incoming(h, _):
        hc = cols_of(h)
        high, low_part = split_state(f_state[:, h].reshape(DH, DH))
        got = mm(twice(q[:, hc]), jnp.concatenate([high, low_part], axis=0), NN)
        o = outw[:, hc] + got * head_b[h]
        outw[:, hc] = o
        acc_sq[...] += o * o
        acc_cr[...] += gain[pl.ds(h, 1), :] * dy[:, hc].astype(F32) * o
        return 0

    late[1].wait()
    small[1].wait()
    for ch in range(CHUNKS):
        gather(f_state, fb_r, ch)
        lax.fori_loop(ch * GROUP, (ch + 1) * GROUP, incoming, 0)

    ones = jnp.ones((HEADS, DH), F32)

    def row_sums(acc):
        return lax.dot_general(
            ones, acc[...], NT, precision=lax.Precision.HIGHEST, preferred_element_type=F32
        )

    sub = lax.broadcasted_iota(jnp.int32, (HEADS, DH), 0)
    squares, crossed = row_sums(acc_sq), row_sums(acc_cr)
    parts = TOK // DH
    sums = jnp.zeros((HEADS, DH), F32)
    for i in range(parts):
        lanes = slice(i * DH, (i + 1) * DH)
        sums = jnp.where(sub == i, squares[:, lanes], sums)
        sums = jnp.where(sub == parts + i, crossed[:, lanes], sums)
    tp_own[...] = sums
    tp_got[t] = sums
    for i in TEAM:
        remote(tp_own, tp_got.at[t], 5, recv_sem.at[2], t_dev(i)).start()
    arrive(tp_got.at[pl.ds(0, PEERS - 1)], recv_sem.at[2])
    sums = tp_got[0]
    for i in range(1, PEERS):
        sums = sums + tp_got[i]
    squares = jnp.concatenate([sums[i:i + 1] for i in range(parts)], axis=1)
    crossed = jnp.concatenate([sums[parts + i:parts + i + 1] for i in range(parts)], axis=1)
    scaled = 1.0 / jnp.sqrt(squares / WIDTH + norm_eps)
    coef = scaled * scaled * scaled * crossed / WIDTH
    stacked = jnp.concatenate(
        [jnp.broadcast_to(scaled, (HEADS, TOK)), jnp.broadcast_to(coef, (HEADS, TOK)),
         jnp.zeros((DH - 2 * HEADS, TOK), F32)], axis=0
    )
    norm_columns = stacked.T
    scale_b[...] = jnp.broadcast_to(norm_columns[:, 0:1], (TOK, DH))
    coef_b[...] = jnp.broadcast_to(norm_columns[:, HEADS:HEADS + 1], (TOK, DH))

    def emit(h, _):
        hc = cols_of(h)
        o = outw[:, hc]
        dyh = dy[:, hc].astype(F32)
        sc = scale_b[...]
        g = (sc * gain[pl.ds(h, 1), :] * dyh - o * coef_b[...]).astype(BF16)
        go[:, hc] = g
        gz_own[pl.ds(h, 1), :] = jnp.sum(dyh * o * sc, axis=0, keepdims=True)
        lifted = (q[:, hc].astype(F32) * head_b[h]).astype(BF16)
        b_loc[:, h] = mm(lifted, g, TN).reshape(COLS, PART, DH)
        return 0

    for ch in range(CHUNKS):
        lax.fori_loop(ch * GROUP, (ch + 1) * GROUP, emit, 0)
        scatter(b_loc, b_got, 6, ba_r, ch)
    gz_got[z] = gz_own[...]
    for i in RING:
        remote(gz_own, gz_got.at[z], 9, recv_sem.at[3], z_dev(i)).start()

    def grads(h, _):
        hc = cols_of(h)
        high, low_part = split_state(f_state[:, h].reshape(DH, DH))
        state = jnp.concatenate([high, low_part], axis=1)
        for i in range(2):
            n = HALF * (i + 1)
            ts = slice(HALF * i, n)
            g = go[ts, hc]
            gp = (mm(g, v[:n, hc], NT) * weights[h, ts, :n]).astype(BF16)
            gps[ts, :n] = gp
            across = mm(twice(g), state, NT) * head_b[h, ts]
            gqs[ts, hc] = mm(gp, k[:n, hc], NN) + across
        for j in range(2):
            rs = slice(HALF * j, TOK)
            ss = slice(HALF * j, HALF * (j + 1))
            gks[ss, hc] = mm(gps[rs, ss], q[rs, hc], TN)
            gvs[ss, hc] = mm(probs[h, rs, ss], go[rs, hc], TN)
        return 0

    lax.fori_loop(0, 3, grads, 0)
    arrive(gz_got.at[pl.ds(0, COLS - 1)], recv_sem.at[3])
    part = gz_got[0]
    for b in range(1, COLS):
        part = part + gz_got[b]
    gx_own[...] = part
    gx_got[x] = part
    for i in LINE:
        remote(gx_own, gx_got.at[x], 10, recv_sem.at[4], x_dev(i)).start()
    scan(
        (b_got, b_ret, b_tot, b_tgot, b_state), 7, (ba_r, bx_r, bb_r), back, (3, 2),
        jnp.where(x <= ROWS - 2, 1.0, 0.0), jnp.where(x <= ROWS - 3, 1.0, 0.0), 1, grads, 3,
    )
    arrive(gx_got.at[pl.ds(0, ROWS - 1)], recv_sem.at[4])
    part = gx_got[0]
    for b in range(1, ROWS):
        part = part + gx_got[b]
    gg_ref[...] = part
    seven = pl.ds(0, COLS - 1)
    sent(thr.at[seven], 0)
    sent(f_got.at[seven], 1)
    sent(row_got, 2)
    sent(f_tgot, 3)
    sent(f_state.at[seven], 4)
    sent(tp_got.at[seven], 5)
    sent(b_got.at[seven], 6)
    sent(b_tgot, 7)
    sent(gz_got.at[seven], 9)
    sent(gx_got.at[pl.ds(0, ROWS - 1)], 10)
    sent(b_state.at[seven], 8)
    for ch in range(CHUNKS):
        gather(b_state, bb_r, ch)


def finish_kernel(
    gq, gkp, gvp, gg, state_ref, columns, k, v, gq_hbm, gk_hbm, gv_hbm, gg_hbm, gk, gv, sem,
):
    stores = []

    def store(src, dst):
        cp = pltpu.make_async_copy(src, dst, sem.at[len(stores)])
        cp.start()
        stores.append(cp)

    store(gq, gq_hbm)
    store(gg, gg_hbm)
    for h in range(HEADS):
        hc = slice(h * DH, (h + 1) * DH)
        at = 2 * HEADS + h
        high, low_part = split_state(state_ref[:, h].reshape(DH, DH))
        decay = columns[:, at:at + 1]
        gk[:, hc] = gkp[:, hc] + mm(twice(v[:, hc]), jnp.concatenate([high, low_part], axis=1), NT) * decay
        store(gk.at[:, hc], gk_hbm.at[:, hc])
        gv[:, hc] = gvp[:, hc] + mm(twice(k[:, hc]), jnp.concatenate([high, low_part], axis=0), NN) * decay
        store(gv.at[:, hc], gv_hbm.at[:, hc])
    for cp in stores:
        cp.wait()


def local(query_input, key_input, value_input, log_decay, norm_gain, cotangent, doc_lengths):
    flat = (TOK, HEADS * DH)
    vmem = pltpu.VMEM
    dma = pltpu.SemaphoreType.DMA
    slices = vmem((COLS, HEADS, PART, DH), F32)
    travel = [slices, slices, vmem((HEADS, PART, DH), F32), vmem((2, HEADS, PART, DH), F32), slices]
    tile = vmem((HEADS, DH), F32)
    tiles = vmem((COLS, HEADS, DH), F32)
    per_head = vmem((HEADS, TOK, DH), F32)
    column = vmem((TOK, DH), F32)
    wide = vmem(flat, F32)
    block = vmem(flat, BF16)
    out = jax.ShapeDtypeStruct(flat, F32)
    tile_out = jax.ShapeDtypeStruct((HEADS, DH), F32)
    anywhere = pl.BlockSpec(memory_space=pl.ANY)
    in_vmem = pl.BlockSpec(memory_space=pltpu.VMEM)
    chunk_sem = dma((CHUNKS,))
    kept = pl.pallas_call(
        kernel,
        out_shape=(wide, wide, wide, tile, slices, column, block, block),
        in_specs=[pl.BlockSpec(memory_space=pltpu.SMEM)] + [anywhere] * 6,
        out_specs=(in_vmem,) * 8,
        scratch_shapes=[
            block, block, block, wide,
            vmem((HEADS, TOK, TOK), F32), vmem((HEADS, TOK, TOK), BF16), vmem((TOK, TOK), BF16),
            vmem((TOK, TOK), F32), vmem((HEADS, TOK), F32), tile,
            vmem((HEADS, TOK), F32), per_head, per_head, per_head, column, column, column, column,
            tile, tiles, tile, vmem((2, HEADS, DH), F32),
            *travel, slices, *travel,
            tile, tiles, tile, tiles, tile, vmem((ROWS, HEADS, DH), F32),
            dma((4 + 2 * CHUNKS,)), dma((11,)), dma((5,)), *([chunk_sem] * 6),
        ],
        compiler_params=pltpu.CompilerParams(
            collective_id=0, has_side_effects=True, vmem_limit_bytes=52 << 20
        ),
        cost_estimate=pl.CostEstimate(flops=5 << 30, bytes_accessed=10 << 20, transcendentals=2 << 20),
        name="attention_backward",
    )(
        doc_lengths, query_input, key_input, value_input, log_decay.T,
        norm_gain.reshape(HEADS, DH), cotangent,
    )
    gq, gk, gv, gg = pl.pallas_call(
        finish_kernel,
        out_shape=(out, out, out, tile_out),
        in_specs=[in_vmem] * 8,
        out_specs=(anywhere,) * 4,
        scratch_shapes=[wide, wide, dma((2 + 2 * HEADS,))],
        compiler_params=pltpu.CompilerParams(vmem_limit_bytes=8 << 20),
        cost_estimate=pl.CostEstimate(flops=1 << 29, bytes_accessed=6 << 20, transcendentals=0),
        name="attention_finish",
    )(*kept)
    return (gq, gk, gv, gg.reshape(HEADS * DH))


def solution(mesh):
    placed = (
        P("ctx", "tp"),
        P("ctx", "tp"),
        P("ctx", "tp"),
        P("ctx", "tp"),
        P("tp"),
        P("ctx", "tp"),
        P(),
    )
    return jax.shard_map(
        local,
        mesh=mesh,
        in_specs=placed,
        out_specs=(P("ctx", "tp"), P("ctx", "tp"), P("ctx", "tp"), P("tp")),
        check_vma=False,
    )
```

```python
import jax
import jax.numpy as jnp
from jax import lax
from jax.experimental import pallas as pl
from jax.experimental.pallas import tpu as pltpu
from jax.sharding import PartitionSpec as P

DH = 128
HEADS = 8
TOK = 512
ROWS = 4
COLS = 8
PEERS = 8
PART = DH // COLS
SIZES = (2, 3, 3)
CHUNKS = len(SIZES)
STARTS = tuple(sum(SIZES[:i]) for i in range(CHUNKS + 1))
HALF = TOK // 2
WIDTH = HEADS * DH * PEERS
norm_eps = 1e-06
MESH = pl.DeviceIdType.MESH
RING = (4, 3, 5, 2, 6, 1, 7)
LINE = (2, 1, 3)
TEAM = (4, 5, 3, 2, 6, 7, 1)
F32 = jnp.float32
BF16 = jnp.bfloat16

NN = (((1,), (0,)), ((), ()))
NT = (((1,), (1,)), ((), ()))
TN = (((0,), (0,)), ((), ()))


def mm(a, b, form):
    return lax.dot_general(a, b, form, preferred_element_type=F32)


def cols_of(h):
    return pl.ds(pl.multiple_of(h * DH, DH), DH)


def split_state(state):
    high = state.astype(BF16)
    return high, (state - high.astype(F32)).astype(BF16)


def twice(a):
    return jnp.concatenate([a, a], axis=1)


def kernel(
    docs, q_hbm, k_hbm, v_hbm, dec_hbm, gain_hbm, dy_hbm,
    gqs, gks, gvs, gg_ref, b_state, columns, k, v,
    q, dy, go, lift, outw, weights, probs, gps, bias, dec, gain,
    cum_rows, cum_b, head_b, tail_b, acc_sq, acc_cr, scale_b, coef_b,
    thr_own, thr, row_own, row_got,
    f_loc, f_got, f_tot, f_tgot, f_ret, f_state,
    b_loc, b_got, b_tot, b_tgot, b_ret,
    tp_own, tp_got, gz_own, gz_got, gx_own, gx_got,
    in_sem, send_sem, recv_sem, fa_r, fx_r, fb_r, ba_r, bx_r, bb_r,
):
    c = lax.axis_index("ctx")
    t = lax.axis_index("tp")
    x = c // COLS
    z = lax.rem(c, COLS)

    def z_dev(i):
        return (x * COLS + lax.rem(z + i, COLS), t)

    def x_dev(i):
        return (lax.rem(x + i, ROWS) * COLS + z, t)

    def t_dev(i):
        return (c, lax.rem(t + i, PEERS))

    def load(i, src, dst):
        cp = pltpu.make_async_copy(src, dst, in_sem.at[i])
        cp.start()
        return cp

    small = [load(0, dec_hbm, dec), load(1, gain_hbm, gain)]

    def load_pair(ch):
        hs = pl.ds(STARTS[ch] * DH, SIZES[ch] * DH)
        return [load(2 + 2 * ch, k_hbm.at[:, hs], k.at[:, hs]), load(3 + 2 * ch, v_hbm.at[:, hs], v.at[:, hs])]

    pair = [load_pair(0)]

    barrier = pltpu.get_barrier_semaphore()
    others = [z_dev(i) for i in RING] + [x_dev(i) for i in LINE] + [t_dev(i) for i in TEAM]
    for other in others:
        pl.semaphore_signal(barrier, inc=1, device_id=other, device_id_type=MESH)

    def remote(src, dst, phase, rs, dev):
        return pltpu.make_async_remote_copy(
            src_ref=src, dst_ref=dst, send_sem=send_sem.at[phase], recv_sem=rs, device_id=dev, device_id_type=MESH
        )

    def arrive(view, rs):
        remote(view, view, 0, rs, others[0]).wait_recv()

    def sent(view, phase):
        remote(view, view, phase, recv_sem.at[0], others[0]).wait_send()

    offset = c * TOK
    pos = offset + lax.broadcasted_iota(jnp.int32, (HEADS, TOK), 1)

    def doc_step(d, carry):
        start, low, low_last = carry
        low = jnp.where(pos >= start, start, low)
        low_last = jnp.where(offset + TOK - 1 >= start, start, low_last)
        return start + docs[d], low, low_last

    zero = jnp.int32(0)
    _, low, low_last = lax.fori_loop(
        0, docs.shape[0], doc_step, (zero, jnp.zeros((HEADS, TOK), jnp.int32), zero)
    )
    lane = lax.broadcasted_iota(jnp.int32, (HEADS, TOK), 1)
    small[0].wait()
    cum = dec[...]
    step = 1
    while step < TOK:
        cum = cum + jnp.where(lane >= step, pltpu.roll(cum, step, 1), 0.0)
        step *= 2
    cum_rows[...] = cum
    head = jnp.where(low < offset, jnp.exp(cum), 0.0)
    tail = jnp.where(pos >= low_last, jnp.exp(cum[:, TOK - 1:] - cum), 0.0)
    through = jnp.broadcast_to(head[:, TOK - 1:], (HEADS, DH))
    thr_own[...] = through
    thr[z] = through
    first = (low - offset).astype(F32)
    stacked = jnp.concatenate(
        [cum, head, tail, first, jnp.zeros((DH - 4 * HEADS, TOK), F32)], axis=0
    )
    columns[...] = stacked.T

    def scatter(loc, got, phase, rs, ch):
        hs = pl.ds(STARTS[ch], SIZES[ch])
        for i in RING:
            p = lax.rem(z + i, COLS)
            remote(loc.at[p, hs], got.at[z, hs], phase, rs.at[ch], z_dev(i)).start()
        got[z, hs] = loc[z, hs]

    def gather(got, rs, ch):
        arrive(got.at[pl.ds(0, COLS - 1), pl.ds(STARTS[ch], SIZES[ch])], rs.at[ch])

    def local_state(h, _):
        hc = cols_of(h)
        decayed = (v[:, hc].astype(F32) * tail_b[h]).astype(BF16)
        f_loc[:, h] = mm(k[:, hc], decayed, TN).reshape(COLS, PART, DH)
        return 0

    for ch in range(CHUNKS):
        for h in range(STARTS[ch], STARTS[ch + 1]):
            at = 2 * HEADS + h
            tail_b[h] = jnp.broadcast_to(columns[:, at:at + 1], (TOK, DH))
        for cp in pair[ch]:
            cp.wait()
        if ch == 0:
            pair += [load_pair(other) for other in range(1, CHUNKS)]
        lax.fori_loop(STARTS[ch], STARTS[ch + 1], local_state, 0)
        if ch == 0:
            pl.semaphore_wait(barrier, len(others))
            for i in RING:
                remote(thr_own, thr.at[z], 0, recv_sem.at[0], z_dev(i)).start()
        scatter(f_loc, f_got, 1, fa_r, ch)
    late = [load(2 + 2 * CHUNKS, q_hbm, q), load(3 + 2 * CHUNKS, dy_hbm, dy)]

    for h in range(HEADS):
        cum_b[h] = jnp.broadcast_to(columns[:, h:h + 1], (TOK, DH))
        at = HEADS + h
        head_b[h] = jnp.broadcast_to(columns[:, at:at + 1], (TOK, DH))
    at = 3 * HEADS
    row = lax.broadcasted_iota(jnp.int32, (TOK, TOK), 0)
    col = lax.broadcasted_iota(jnp.int32, (TOK, TOK), 1)
    begin = columns[:, at:at + 1].astype(jnp.int32)
    bias[...] = jnp.where((col >= begin) & (col <= row), 0.0, -1e30)
    late[0].wait()

    def within(h, _):
        hc = cols_of(h)
        for i in range(2):
            n = HALF * (i + 1)
            ts = slice(HALF * i, n)
            scores = mm(q[ts, hc], k[:n, hc], NT)
            decay = jnp.concatenate([cum_b[h, ts]] * (n // DH), axis=1)
            spread = decay - cum_rows[pl.ds(h, 1), :n]
            w = jnp.exp(spread + bias[ts, :n])
            p = (scores * w).astype(BF16)
            weights[h, ts, :n] = w
            probs[h, ts, :n] = p
            outw[ts, hc] = mm(p, v[:n, hc], NN)
        return 0

    def scan_local(got, ret, tot, ch, order):
        def body(h, _):
            carry = jnp.zeros((PART, DH), F32)
            for b in order:
                ret[b, h] = carry
                carry = thr[b, pl.ds(h, 1), :] * carry + got[b, h]
            tot[h] = carry
            return 0

        lax.fori_loop(STARTS[ch], STARTS[ch + 1], body, 0)

    def scan_rows(ret, tgot, ch, order, near, far, at):
        def body(h, _):
            enter = tgot[0, h] * near + (row_got[at, pl.ds(h, 1), :] * far) * tgot[1, h]
            for b in order:
                ret[b, h] = ret[b, h] + enter
                enter = thr[b, pl.ds(h, 1), :] * enter
            return 0

        lax.fori_loop(STARTS[ch], STARTS[ch + 1], body, 0)

    def send_totals(tot, tgot, phase, rs, ch, steps):
        hs = pl.ds(STARTS[ch], SIZES[ch])
        for j, i in reversed(list(enumerate(steps))):
            remote(tot.at[hs], tgot.at[j, hs], phase, rs.at[ch], x_dev(i)).start()

    forth = range(COLS)
    back = range(COLS - 1, -1, -1)

    lax.fori_loop(0, 3, within, 0)
    arrive(thr.at[pl.ds(0, COLS - 1)], recv_sem.at[0])
    total = thr[0]
    for b in range(1, COLS):
        total = total * thr[b]
    row_own[...] = total
    for j, i in enumerate((1, 3)):
        remote(row_own, row_got.at[j], 2, recv_sem.at[1], x_dev(i)).start()

    def scan(state, phase, sems, order, steps, near, far, at, fill, first_fill):
        got, ret, tot, tgot, back_to = state
        a_r, x_r, b_r = sems

        def give(ch):
            arrive(tgot.at[:, pl.ds(STARTS[ch], SIZES[ch])], x_r.at[ch])
            scan_rows(ret, tgot, ch, order, near, far, at)
            scatter(ret, back_to, phase + 1, b_r, ch)

        for ch in range(CHUNKS):
            gather(got, a_r, ch)
            scan_local(got, ret, tot, ch, order)
            send_totals(tot, tgot, phase, x_r, ch, steps)
            lax.fori_loop(first_fill + ch, first_fill + ch + 1, fill, 0)
            if ch == 0:
                arrive(row_got, recv_sem.at[1]) if at == 0 else None
            if ch >= 1:
                give(ch - 1)
        give(CHUNKS - 1)
        lax.fori_loop(first_fill + CHUNKS, HEADS, fill, 0)

    scan(
        (f_got, f_ret, f_tot, f_tgot, f_state), 3, (fa_r, fx_r, fb_r), forth, (1, 2),
        jnp.where(x >= 1, 1.0, 0.0), jnp.where(x >= 2, 1.0, 0.0), 0, within, 3,
    )

    acc_sq[...] = jnp.zeros_like(acc_sq)
    acc_cr[...] = jnp.zeros_like(acc_cr)

    def raised(h, _):
        hc = cols_of(h)
        lift[:, hc] = (q[:, hc].astype(F32) * head_b[h]).astype(BF16)
        return 0

    def incoming(h, _):
        hc = cols_of(h)
        high, low_part = split_state(f_state[:, h].reshape(DH, DH))
        got = mm(twice(q[:, hc]), jnp.concatenate([high, low_part], axis=0), NN)
        o = outw[:, hc] + got * head_b[h]
        outw[:, hc] = o
        acc_sq[...] += o * o
        acc_cr[...] += gain[pl.ds(h, 1), :] * dy[:, hc].astype(F32) * o
        return 0

    late[1].wait()
    small[1].wait()
    for ch in range(CHUNKS):
        gather(f_state, fb_r, ch)
        lax.fori_loop(STARTS[ch], STARTS[ch + 1], incoming, 0)

    ones = jnp.ones((HEADS, DH), F32)

    def row_sums(acc):
        return lax.dot_general(
            ones, acc[...], NT, precision=lax.Precision.HIGHEST, preferred_element_type=F32
        )

    sub = lax.broadcasted_iota(jnp.int32, (HEADS, DH), 0)
    squares, crossed = row_sums(acc_sq), row_sums(acc_cr)
    parts = TOK // DH
    sums = jnp.zeros((HEADS, DH), F32)
    for i in range(parts):
        lanes = slice(i * DH, (i + 1) * DH)
        sums = jnp.where(sub == i, squares[:, lanes], sums)
        sums = jnp.where(sub == parts + i, crossed[:, lanes], sums)
    tp_own[...] = sums
    tp_got[t] = sums
    for i in TEAM:
        remote(tp_own, tp_got.at[t], 5, recv_sem.at[2], t_dev(i)).start()
    lax.fori_loop(0, HEADS, raised, 0)
    arrive(tp_got.at[pl.ds(0, PEERS - 1)], recv_sem.at[2])
    sums = tp_got[0]
    for i in range(1, PEERS):
        sums = sums + tp_got[i]
    squares = jnp.concatenate([sums[i:i + 1] for i in range(parts)], axis=1)
    crossed = jnp.concatenate([sums[parts + i:parts + i + 1] for i in range(parts)], axis=1)
    scaled = 1.0 / jnp.sqrt(squares / WIDTH + norm_eps)
    coef = scaled * scaled * scaled * crossed / WIDTH
    stacked = jnp.concatenate(
        [jnp.broadcast_to(scaled, (HEADS, TOK)), jnp.broadcast_to(coef, (HEADS, TOK)),
         jnp.zeros((DH - 2 * HEADS, TOK), F32)], axis=0
    )
    norm_columns = stacked.T
    scale_b[...] = jnp.broadcast_to(norm_columns[:, 0:1], (TOK, DH))
    coef_b[...] = jnp.broadcast_to(norm_columns[:, HEADS:HEADS + 1], (TOK, DH))

    def emit(h, _):
        hc = cols_of(h)
        o = outw[:, hc]
        dyh = dy[:, hc].astype(F32)
        sc = scale_b[...]
        g = (sc * gain[pl.ds(h, 1), :] * dyh - o * coef_b[...]).astype(BF16)
        go[:, hc] = g
        b_loc[:, h] = mm(lift[:, hc], g, TN).reshape(COLS, PART, DH)
        return 0

    for ch in range(CHUNKS):
        lax.fori_loop(STARTS[ch], STARTS[ch + 1], emit, 0)
        scatter(b_loc, b_got, 6, ba_r, ch)

    def gain_sum(h, _):
        hc = cols_of(h)
        part = dy[:, hc].astype(F32) * outw[:, hc] * scale_b[...]
        gz_own[pl.ds(h, 1), :] = jnp.sum(part, axis=0, keepdims=True)
        return 0

    lax.fori_loop(0, HEADS, gain_sum, 0)
    gz_got[z] = gz_own[...]
    for i in RING:
        remote(gz_own, gz_got.at[z], 9, recv_sem.at[3], z_dev(i)).start()

    def grads(h, _):
        hc = cols_of(h)
        high, low_part = split_state(f_state[:, h].reshape(DH, DH))
        state = jnp.concatenate([high, low_part], axis=1)
        for i in range(2):
            n = HALF * (i + 1)
            ts = slice(HALF * i, n)
            g = go[ts, hc]
            gp = (mm(g, v[:n, hc], NT) * weights[h, ts, :n]).astype(BF16)
            gps[ts, :n] = gp
            across = mm(twice(g), state, NT) * head_b[h, ts]
            gqs[ts, hc] = mm(gp, k[:n, hc], NN) + across
        for j in range(2):
            rs = slice(HALF * j, TOK)
            ss = slice(HALF * j, HALF * (j + 1))
            gks[ss, hc] = mm(gps[rs, ss], q[rs, hc], TN)
            gvs[ss, hc] = mm(probs[h, rs, ss], go[rs, hc], TN)
        return 0

    lax.fori_loop(0, 3, grads, 0)
    arrive(gz_got.at[pl.ds(0, COLS - 1)], recv_sem.at[3])
    part = gz_got[0]
    for b in range(1, COLS):
        part = part + gz_got[b]
    gx_own[...] = part
    gx_got[x] = part
    for i in LINE:
        remote(gx_own, gx_got.at[x], 10, recv_sem.at[4], x_dev(i)).start()
    scan(
        (b_got, b_ret, b_tot, b_tgot, b_state), 7, (ba_r, bx_r, bb_r), back, (3, 2),
        jnp.where(x <= ROWS - 2, 1.0, 0.0), jnp.where(x <= ROWS - 3, 1.0, 0.0), 1, grads, 3,
    )
    arrive(gx_got.at[pl.ds(0, ROWS - 1)], recv_sem.at[4])
    part = gx_got[0]
    for b in range(1, ROWS):
        part = part + gx_got[b]
    gg_ref[...] = part
    seven = pl.ds(0, COLS - 1)
    sent(thr.at[seven], 0)
    sent(f_got.at[seven], 1)
    sent(row_got, 2)
    sent(f_tgot, 3)
    sent(f_state.at[seven], 4)
    sent(tp_got.at[seven], 5)
    sent(b_got.at[seven], 6)
    sent(b_tgot, 7)
    sent(gz_got.at[seven], 9)
    sent(gx_got.at[pl.ds(0, ROWS - 1)], 10)
    sent(b_state.at[seven], 8)
    for ch in range(CHUNKS):
        gather(b_state, bb_r, ch)


def finish_kernel(
    gq, gkp, gvp, gg, state_ref, columns, k, v, gq_hbm, gk_hbm, gv_hbm, gg_hbm, gk, gv, sem,
):
    stores = []

    def store(src, dst):
        cp = pltpu.make_async_copy(src, dst, sem.at[len(stores)])
        cp.start()
        stores.append(cp)

    store(gq, gq_hbm)
    store(gg, gg_hbm)
    for h in range(HEADS):
        hc = slice(h * DH, (h + 1) * DH)
        at = 2 * HEADS + h
        high, low_part = split_state(state_ref[:, h].reshape(DH, DH))
        decay = columns[:, at:at + 1]
        gk[:, hc] = gkp[:, hc] + mm(twice(v[:, hc]), jnp.concatenate([high, low_part], axis=1), NT) * decay
        store(gk.at[:, hc], gk_hbm.at[:, hc])
        gv[:, hc] = gvp[:, hc] + mm(twice(k[:, hc]), jnp.concatenate([high, low_part], axis=0), NN) * decay
        store(gv.at[:, hc], gv_hbm.at[:, hc])
    for cp in stores:
        cp.wait()


def local(query_input, key_input, value_input, log_decay, norm_gain, cotangent, doc_lengths):
    flat = (TOK, HEADS * DH)
    vmem = pltpu.VMEM
    dma = pltpu.SemaphoreType.DMA
    slices = vmem((COLS, HEADS, PART, DH), F32)
    travel = [slices, slices, vmem((HEADS, PART, DH), F32), vmem((2, HEADS, PART, DH), F32), slices]
    tile = vmem((HEADS, DH), F32)
    tiles = vmem((COLS, HEADS, DH), F32)
    per_head = vmem((HEADS, TOK, DH), F32)
    column = vmem((TOK, DH), F32)
    wide = vmem(flat, F32)
    block = vmem(flat, BF16)
    out = jax.ShapeDtypeStruct(flat, F32)
    tile_out = jax.ShapeDtypeStruct((HEADS, DH), F32)
    anywhere = pl.BlockSpec(memory_space=pl.ANY)
    in_vmem = pl.BlockSpec(memory_space=pltpu.VMEM)
    chunk_sem = dma((CHUNKS,))
    kept = pl.pallas_call(
        kernel,
        out_shape=(wide, wide, wide, tile, slices, column, block, block),
        in_specs=[pl.BlockSpec(memory_space=pltpu.SMEM)] + [anywhere] * 6,
        out_specs=(in_vmem,) * 8,
        scratch_shapes=[
            block, block, block, block, wide,
            vmem((HEADS, TOK, TOK), F32), vmem((HEADS, TOK, TOK), BF16), vmem((TOK, TOK), BF16),
            vmem((TOK, TOK), F32), vmem((HEADS, TOK), F32), tile,
            vmem((HEADS, TOK), F32), per_head, per_head, per_head, column, column, column, column,
            tile, tiles, tile, vmem((2, HEADS, DH), F32),
            *travel, slices, *travel,
            tile, tiles, tile, tiles, tile, vmem((ROWS, HEADS, DH), F32),
            dma((4 + 2 * CHUNKS,)), dma((11,)), dma((5,)), *([chunk_sem] * 6),
        ],
        compiler_params=pltpu.CompilerParams(
            collective_id=0, has_side_effects=True, vmem_limit_bytes=52 << 20
        ),
        cost_estimate=pl.CostEstimate(flops=5 << 30, bytes_accessed=10 << 20, transcendentals=2 << 20),
        name="attention_backward",
    )(
        doc_lengths, query_input, key_input, value_input, log_decay.T,
        norm_gain.reshape(HEADS, DH), cotangent,
    )
    gq, gk, gv, gg = pl.pallas_call(
        finish_kernel,
        out_shape=(out, out, out, tile_out),
        in_specs=[in_vmem] * 8,
        out_specs=(anywhere,) * 4,
        scratch_shapes=[wide, wide, dma((2 + 2 * HEADS,))],
        compiler_params=pltpu.CompilerParams(vmem_limit_bytes=8 << 20),
        cost_estimate=pl.CostEstimate(flops=1 << 29, bytes_accessed=6 << 20, transcendentals=0),
        name="attention_finish",
    )(*kept)
    return (gq, gk, gv, gg.reshape(HEADS * DH))


def solution(mesh):
    placed = (
        P("ctx", "tp"),
        P("ctx", "tp"),
        P("ctx", "tp"),
        P("ctx", "tp"),
        P("tp"),
        P("ctx", "tp"),
        P(),
    )
    return jax.shard_map(
        local,
        mesh=mesh,
        in_specs=placed,
        out_specs=(P("ctx", "tp"), P("ctx", "tp"), P("ctx", "tp"), P("tp")),
        check_vma=False,
    )
```
